256 devices in a mesh: dp: 32 (over z_hi, x, core), tensor: 8 (over z_lo, y).
Axes of the slice: x: 4, y: 4, z: 8 (z_hi: 4, z_lo: 2; z = z_hi * 2 + z_lo), core: 2. Of those that a mesh axis runs over, the one named last changes fastest.
Arguments:
- resp_queries: bfloat16 [8192, 8192], P('dp', 'tensor'), may hold values from -80 to 80
- resp_keys: bfloat16 [8192, 1024], P('dp', 'tensor'), may hold values from -7 to 7
- resp_values: bfloat16 [8192, 1024], P('dp', 'tensor'), may hold values from -6 to 6
- prompt_keys: bfloat16 [4096, 4, 1024], P(('dp', 'tensor')), may hold values from -6 to 6
- prompt_values: bfloat16 [4096, 4, 1024], P(('dp', 'tensor')), may hold values from -6 to 6
- out_grad: bfloat16 [8192, 8192], P('dp', 'tensor'), may hold values from -6 to 6
- lengths: int32 [64], P('dp'), may hold values from 1 to 128, as said below
- prompt_of: int32 [32], replicated, may hold values from 0 to 3, as said below
Outputs:
- attn_out: bfloat16 [8192, 8192], P('dp', 'tensor')
- grad_queries: bfloat16 [8192, 8192], P('dp', 'tensor')
- grad_resp_keys: bfloat16 [8192, 1024], P('dp', 'tensor')
- grad_resp_values: bfloat16 [8192, 1024], P('dp', 'tensor')
- grad_prompt_keys: bfloat16 [4096, 4, 1024], P(('dp', 'tensor'))
- grad_prompt_values: bfloat16 [4096, 4, 1024], P(('dp', 'tensor'))
The draws below stay inside these ranges and needn't reach their ends.
Inputs may be any that keep to these rules, and one draw needn't show every extreme that they name: `prompt_of`: each prompt index is named by exactly 8 entries. `lengths`: some response has all 128 tokens live in every draw.
All inputs are finite; a program needn't handle non-finite values.
Results may differ from the reference program's by a relative error of at most 0.007.
Values may be sent and summed in bfloat16 or wider, within the bound.
A program may use at most 64 MiB of HBM per device.

```python
import jax
import jax.numpy as jnp
from jax import lax

HEADS = 64
KV_HEADS = 8
HEAD_DIM = 128
RESP_LEN = 128
PROMPT_LEN = 4096
RESP_DEV = 2
GROUP_RESP = 16
RESPONSES = 64
PROMPTS = 4
N_DP = 32


def base_keys(key):
    raw = jax.random.normal(jax.random.fold_in(key, 11), (RESPONSES * RESP_LEN, KV_HEADS * HEAD_DIM), jnp.float32)
    return jnp.clip(raw, -6.0, 6.0)


def draw_resp_keys(key, part):
    keys_now = base_keys(key)
    return keys_now.astype(jnp.bfloat16)


def draw_resp_queries(key, part):
    key = jax.random.fold_in(key, 5)
    total_rows = RESPONSES * RESP_LEN
    queries = jnp.clip(jax.random.normal(key, (total_rows, HEADS * HEAD_DIM), jnp.float32), -6.0, 6.0)
    return queries.astype(jnp.bfloat16)


def draw_lengths(key, part):
    key = jax.random.fold_in(key, 13)
    drawn = jax.random.randint(key, (RESPONSES,), 1, RESP_LEN + 1)
    where_full = jax.random.randint(jax.random.fold_in(key, 1), (), 0, RESPONSES)
    return drawn.at[where_full].set(RESP_LEN).astype(jnp.int32)


def draw_prompt_of(key, part):
    key = jax.random.fold_in(key, 17)
    order = jax.random.permutation(key, N_DP)
    return (order // (GROUP_RESP // RESP_DEV)).astype(jnp.int32)


def block_levels(rng, dims, pieces, least, top_value):
    gain, own = 1.0, jax.random.fold_in(rng, 6)
    for axis_at, shards_of in pieces:
        steps = jnp.exp(jax.random.uniform(jax.random.fold_in(own, axis_at), (shards_of,), jnp.float32, least / len(pieces), top_value / len(pieces)))
        gain = gain * jnp.repeat(steps, dims[axis_at] // shards_of).reshape([-1 if axis == axis_at else 1 for axis in range(len(dims))])
    return gain


def bell_draw(key, dims, deviation, limit, pieces=(), held_as=jnp.bfloat16):
    factor_of = block_levels(key, dims, pieces, -0.22, 0.18) if pieces else 1.0
    values = jax.random.normal(key, dims, jnp.float32) * deviation * factor_of
    return jnp.minimum(jnp.maximum(values, -limit), limit).astype(held_as)


def setup_inputs(seed: int = 0) -> dict:
    splits = jax.random.split(jax.random.key(seed), 9)
    resp_queries = draw_resp_queries(jax.random.fold_in(splits[8], 71), 0)
    resp_keys = draw_resp_keys(jax.random.fold_in(splits[8], 71), 0)
    resp_values = bell_draw(splits[2], (RESPONSES * RESP_LEN, KV_HEADS * HEAD_DIM), 1.0, 6.0, ((0, 32), (1, 8)))
    prompt_keys = bell_draw(splits[3], (PROMPT_LEN, PROMPTS, KV_HEADS * HEAD_DIM), 1.0, 6.0, ((0, 256),))
    prompt_values = bell_draw(splits[4], (PROMPT_LEN, PROMPTS, KV_HEADS * HEAD_DIM), 1.0, 6.0, ((0, 256),))
    out_grad = bell_draw(splits[5], (RESPONSES * RESP_LEN, HEADS * HEAD_DIM), 1.0, 6.0, ((0, 32), (1, 8)))
    lengths = draw_lengths(jax.random.fold_in(splits[8], 71), 0)
    prompt_of = draw_prompt_of(jax.random.fold_in(splits[8], 71), 0)
    return dict(resp_queries=resp_queries, resp_keys=resp_keys, resp_values=resp_values, prompt_keys=prompt_keys, prompt_values=prompt_values, out_grad=out_grad, lengths=lengths, prompt_of=prompt_of)


def head_pass(query_rows, prompt_k, prompt_v, own_k, own_v, grad_out, length):
    num_rows = query_rows.shape[0]
    prompt_span = prompt_k.shape[0]
    all_keys = jnp.concatenate([prompt_k, own_k], 0)
    all_values = jnp.concatenate([prompt_v, own_v], 0)
    scale_now = HEAD_DIM ** -0.5
    column_pos = lax.broadcasted_iota(jnp.int32, (num_rows, prompt_span + num_rows), 1) - prompt_span
    row_pos = lax.broadcasted_iota(jnp.int32, (num_rows, prompt_span + num_rows), 0)
    allowed = (column_pos < 0) | ((column_pos <= row_pos) & (column_pos < length))
    valid_rows = lax.broadcasted_iota(jnp.int32, (num_rows, 1), 0) < length
    scores = jnp.dot(query_rows, all_keys.T, preferred_element_type=jnp.float32) * scale_now
    scores = jnp.where(allowed, scores, -1e30)
    row_max = jnp.max(scores, axis=1, keepdims=True)
    exp_terms = jnp.exp(scores - row_max)
    probs = exp_terms / jnp.sum(exp_terms, axis=1, keepdims=True)
    weights = probs.astype(jnp.bfloat16)
    mixed = jnp.dot(weights, all_values, preferred_element_type=jnp.float32)
    mixed = jnp.where(valid_rows, mixed, 0.0).astype(jnp.bfloat16)
    masked_grad = jnp.where(valid_rows, grad_out, jnp.zeros_like(grad_out))
    value_terms = jnp.dot(weights.T, masked_grad, preferred_element_type=jnp.float32)
    grad_w = jnp.dot(masked_grad, all_values.T, preferred_element_type=jnp.float32)
    row_inner = jnp.sum(grad_w * probs, axis=1, keepdims=True)
    dscore = (probs * (grad_w - row_inner) * scale_now).astype(jnp.bfloat16)
    grad_q = jnp.dot(dscore, all_keys, preferred_element_type=jnp.float32).astype(jnp.bfloat16)
    key_terms = jnp.dot(dscore.T, query_rows, preferred_element_type=jnp.float32)
    return (mixed, grad_q, key_terms[:prompt_span], value_terms[:prompt_span],
            key_terms[prompt_span:], value_terms[prompt_span:])


def head_cols(source, index_now):
    start = (index_now * HEAD_DIM).astype(jnp.int32)
    return lax.dynamic_slice_in_dim(source, start, HEAD_DIM, 1)


def put_cols(target, piece, index_now):
    start = (index_now * HEAD_DIM).astype(jnp.int32)
    return lax.dynamic_update_slice_in_dim(target, piece, start, 1)


def device_pass(resp_queries, resp_keys, resp_values, span_k, span_v, out_grad, lengths):
    resp_count = lengths.shape[0]
    resp_len = resp_queries.shape[0] // resp_count
    q_count = resp_queries.shape[1] // HEAD_DIM
    kv_count = resp_keys.shape[1] // HEAD_DIM
    group_size = q_count // kv_count
    span_rows = span_k.shape[0]
    batched = jax.vmap(head_pass, in_axes=(0, None, None, 0, 0, 0, 0))

    def by_resp(source):
        return source.reshape(resp_count, resp_len, HEAD_DIM)

    def head_step(head_idx, state_now):
        mixed, grad_q, grad_pkeys, grad_pvalues, grad_rkeys, grad_rvalues = state_now
        head_idx = head_idx.astype(jnp.int32)
        kv_idx = head_idx // group_size
        results = batched(by_resp(head_cols(resp_queries, head_idx)), head_cols(span_k, kv_idx),
                          head_cols(span_v, kv_idx), by_resp(head_cols(resp_keys, kv_idx)),
                          by_resp(head_cols(resp_values, kv_idx)), by_resp(head_cols(out_grad, head_idx)), lengths)
        mixed = put_cols(mixed, results[0].reshape(-1, HEAD_DIM), head_idx)
        grad_q = put_cols(grad_q, results[1].reshape(-1, HEAD_DIM), head_idx)
        grad_pkeys = put_cols(grad_pkeys, head_cols(grad_pkeys, kv_idx) + jnp.sum(results[2], 0), kv_idx)
        grad_pvalues = put_cols(grad_pvalues, head_cols(grad_pvalues, kv_idx) + jnp.sum(results[3], 0), kv_idx)
        grad_rkeys = put_cols(grad_rkeys, head_cols(grad_rkeys, kv_idx) + results[4].reshape(-1, HEAD_DIM), kv_idx)
        grad_rvalues = put_cols(grad_rvalues, head_cols(grad_rvalues, kv_idx) + results[5].reshape(-1, HEAD_DIM), kv_idx)
        return (mixed, grad_q, grad_pkeys, grad_pvalues, grad_rkeys, grad_rvalues)

    initial = (jnp.zeros(resp_queries.shape, jnp.bfloat16), jnp.zeros(resp_queries.shape, jnp.bfloat16),
               jnp.zeros((span_rows, resp_keys.shape[1]), jnp.float32),
               jnp.zeros((span_rows, resp_keys.shape[1]), jnp.float32),
               jnp.zeros(resp_keys.shape, jnp.float32), jnp.zeros(resp_keys.shape, jnp.float32))
    return lax.fori_loop(0, q_count, head_step, initial)


def reference(resp_queries, resp_keys, resp_values, prompt_keys, prompt_values, out_grad, lengths, prompt_of):
    rows_dev = RESP_DEV * RESP_LEN
    queries_dev = resp_queries.reshape(N_DP, rows_dev, -1)
    keys_dev = resp_keys.reshape(N_DP, rows_dev, -1)
    values_dev = resp_values.reshape(N_DP, rows_dev, -1)
    grads_dev = out_grad.reshape(N_DP, rows_dev, -1)
    lengths_dev = lengths.reshape(N_DP, RESP_DEV)
    prompt_kall = jnp.transpose(prompt_keys, (1, 0, 2))
    prompt_vall = jnp.transpose(prompt_values, (1, 0, 2))

    def one_device(inputs):
        q_dev, k_dev, v_dev, g_dev, l_dev, owner = inputs
        span_k = lax.dynamic_index_in_dim(prompt_kall, owner.astype(jnp.int32), 0, keepdims=False)
        span_v = lax.dynamic_index_in_dim(prompt_vall, owner.astype(jnp.int32), 0, keepdims=False)
        return device_pass(q_dev, k_dev, v_dev, span_k, span_v, g_dev, l_dev)

    mixed, grad_q, grad_pkeys, grad_pvalues, grad_rkeys, grad_rvalues = lax.map(
        one_device, (queries_dev, keys_dev, values_dev, grads_dev, lengths_dev, prompt_of))
    sum_pkeys = jax.ops.segment_sum(grad_pkeys, prompt_of, PROMPTS)
    sum_pvalues = jax.ops.segment_sum(grad_pvalues, prompt_of, PROMPTS)
    total_rows = RESPONSES * RESP_LEN
    return (mixed.reshape(total_rows, -1), grad_q.reshape(total_rows, -1),
            grad_rkeys.reshape(total_rows, -1).astype(jnp.bfloat16),
            grad_rvalues.reshape(total_rows, -1).astype(jnp.bfloat16),
            jnp.transpose(sum_pkeys, (1, 0, 2)).astype(jnp.bfloat16),
            jnp.transpose(sum_pvalues, (1, 0, 2)).astype(jnp.bfloat16))
```

```python
import jax
import jax.numpy as jnp
from jax import lax
from jax.experimental import pallas as pl
from jax.experimental.pallas import tpu as pltpu
from jax.sharding import PartitionSpec as P

D = 128
F32 = jnp.float32
BF16 = jnp.bfloat16
SCALE = D ** -0.5
LOG2E = 1.4426950408889634
TKF, TRF, TKB, TRB = 2048, 256, 512, 1024


def dot_nt(a, b):
    return lax.dot_general(a, b, (((1,), (1,)), ((), ())), preferred_element_type=F32)


def dot_nn(a, b):
    return jnp.dot(a, b, preferred_element_type=F32)


def own_mask(len_ref, cols, resp_rows, dev_rows):
    key = lax.broadcasted_iota(jnp.int32, (dev_rows, cols), 0)
    row = lax.broadcasted_iota(jnp.int32, (dev_rows, cols), 1) % dev_rows
    length = jnp.where(key < resp_rows, len_ref[0], len_ref[1])
    return (key // resp_rows == row // resp_rows) & (key <= row) & (key % resp_rows < length)


def attn_kernel(q_ref, k_ref, v_ref, rk_ref, rv_ref, g_ref, len_ref,
                o_ref, dq_ref, drk_ref, drv_ref, dk_ref, dv_ref,
                qa, ga, m_s, l_s, d_s, ot, kt, vt, acc_k, acc_v):
    rows = q_ref.shape[0]
    heads = q_ref.shape[1] // D
    half = rows // 2
    span = k_ref.shape[0]
    row_ids = lax.broadcasted_iota(jnp.int32, (rows, D), 0)
    live = (row_ids % half) < jnp.where(row_ids < half, len_ref[0], len_ref[1])
    for h in range(heads):
        qa[pl.ds(h * rows, rows)] = q_ref[:, h * D:(h + 1) * D]
        g = g_ref[:, h * D:(h + 1) * D]
        ga[pl.ds(h * rows, rows)] = jnp.where(live, g, jnp.zeros_like(g))

    mask_f = own_mask(len_ref, TRF, half, rows)
    rvt = rv_ref[...].T

    def own_fwd(j, _):
        blk = pl.ds(j * TRF, TRF)
        s = jnp.where(mask_f, dot_nt(rk_ref[...], qa[blk]) * (SCALE * LOG2E), -1e30)
        m = jnp.max(s, axis=0, keepdims=True)
        e = jnp.exp2(s - m)
        m_s[:, blk] = m
        l_s[:, blk] = jnp.sum(e, axis=0, keepdims=True)
        ot[:, blk] = dot_nn(rvt, e.astype(BF16))
        return 0

    lax.fori_loop(0, heads * rows // TRF, own_fwd, 0)

    def fwd_chunk(i, _):
        ks = k_ref[pl.ds(i * TKF, TKF)]
        vt[...] = v_ref[pl.ds(i * TKF, TKF)].T
        kt[:, pl.ds(i * TKF, TKF)] = ks.T

        def fwd_rows(j, _):
            blk = pl.ds(j * TRF, TRF)
            s = dot_nt(k_ref[pl.ds(i * TKF, TKF)], qa[blk]) * (SCALE * LOG2E)
            m_old = m_s[:, blk]
            m = jnp.maximum(m_old, jnp.max(s, axis=0, keepdims=True))
            e = jnp.exp2(s - m)
            alpha = jnp.exp2(m_old - m)
            m_s[:, blk] = m
            l_s[:, blk] = l_s[:, blk] * alpha + jnp.sum(e, axis=0, keepdims=True)
            ot[:, blk] = ot[:, blk] * alpha + dot_nn(vt[...], e.astype(BF16))
            return 0

        lax.fori_loop(0, heads * rows // TRF, fwd_rows, 0)
        return 0

    lax.fori_loop(0, span // TKF, fwd_chunk, 0)

    for h in range(heads):
        blk = pl.ds(h * rows, rows)
        l = l_s[:, blk]
        o = ot[:, blk] / l
        d_s[:, blk] = jnp.sum(o * ga[blk].T.astype(F32), axis=0, keepdims=True)
        m_s[:, blk] = m_s[:, blk] + jnp.log2(l)
        o_ref[:, h * D:(h + 1) * D] = jnp.where(live, o.T, 0.0).astype(BF16)

    ot[...] = jnp.zeros_like(ot)
    mask_b = own_mask(len_ref, TRB, half, rows)
    rkt = rk_ref[...].T

    def bwd_block(ks, vs, kts, blk, mask):
        qb, gb = qa[blk], ga[blk]
        s = dot_nt(ks, qb) * (SCALE * LOG2E)
        p = jnp.exp2(s - m_s[:, blk])
        if mask is not None:
            p = jnp.where(mask, p, 0.0)
        dp = dot_nt(vs, gb)
        ds = (p * (dp - d_s[:, blk])).astype(BF16)
        dv = dot_nn(p.astype(BF16), gb)
        dk = dot_nn(ds, qb)
        ot[:, blk] += dot_nn(kts, ds)
        return dk, dv

    acc_k[...] = jnp.zeros_like(acc_k)
    acc_v[...] = jnp.zeros_like(acc_v)

    def own_bwd(j, _):
        dk, dv = bwd_block(rk_ref[...], rv_ref[...], rkt, pl.ds(j * TRB, TRB), mask_b)
        acc_k[:rows] += dk
        acc_v[:rows] += dv
        return 0

    lax.fori_loop(0, heads * rows // TRB, own_bwd, 0)
    drk_ref[...] = (acc_k[:rows] * SCALE).astype(BF16)
    drv_ref[...] = acc_v[:rows].astype(BF16)

    def bwd_chunk(i, _):
        cur = pl.ds(i * TKB, TKB)
        acc_k[...] = jnp.zeros_like(acc_k)
        acc_v[...] = jnp.zeros_like(acc_v)

        def bwd_rows(j, _):
            dk, dv = bwd_block(k_ref[cur], v_ref[cur], kt[:, cur], pl.ds(j * TRB, TRB), None)
            acc_k[...] += dk
            acc_v[...] += dv
            return 0

        lax.fori_loop(0, heads * rows // TRB, bwd_rows, 0)
        dk_ref[cur] = (acc_k[...] * SCALE).astype(BF16)
        dv_ref[cur] = acc_v[...].astype(BF16)
        return 0

    lax.fori_loop(0, span // TKB, bwd_chunk, 0)

    for h in range(heads):
        dq_ref[:, h * D:(h + 1) * D] = (ot[:, h * rows:(h + 1) * rows] * SCALE).T.astype(BF16)


def attention(q, k, v, rk, rv, g, lengths):
    rows, width = q.shape
    total = rows * width // D
    span = k.shape[0]
    vm = pl.BlockSpec(memory_space=pltpu.VMEM)
    return pl.pallas_call(
        attn_kernel,
        out_shape=(
            jax.ShapeDtypeStruct(q.shape, BF16),
            jax.ShapeDtypeStruct(q.shape, BF16),
            jax.ShapeDtypeStruct(rk.shape, BF16),
            jax.ShapeDtypeStruct(rk.shape, BF16),
            jax.ShapeDtypeStruct(k.shape, BF16),
            jax.ShapeDtypeStruct(k.shape, BF16),
        ),
        in_specs=[vm] * 6 + [pl.BlockSpec(memory_space=pltpu.SMEM)],
        out_specs=(vm,) * 6,
        scratch_shapes=[
            pltpu.VMEM((total, D), BF16), pltpu.VMEM((total, D), BF16),
            pltpu.VMEM((1, total), F32), pltpu.VMEM((1, total), F32), pltpu.VMEM((1, total), F32),
            pltpu.VMEM((D, total), F32), pltpu.VMEM((D, span), BF16), pltpu.VMEM((D, TKF), BF16),
            pltpu.VMEM((TKB, D), F32), pltpu.VMEM((TKB, D), F32),
        ],
        compiler_params=pltpu.CompilerParams(vmem_limit_bytes=56 * 2 ** 20),
        cost_estimate=pl.CostEstimate(flops=14 * total * span * D, bytes_accessed=6 * 2 ** 20, transcendentals=2 * total * span),
    )(q, k, v, rk, rv, g, lengths)


def local(
    resp_queries, resp_keys, resp_values, prompt_keys, prompt_values, out_grad, lengths, prompt_of
):
    ranks = lax.axis_size("tensor")
    dp_count = lax.axis_size("dp")
    rows_here, prompt_count, full_width = prompt_keys.shape
    head_width = resp_keys.shape[1]
    block_rows = rows_here * ranks
    span_len = block_rows * dp_count
    block_k, block_v = (
        lax.all_to_all(
            prompt_keys.reshape(rows_here, prompt_count, ranks, head_width),
            "tensor",
            split_axis=2,
            concat_axis=0,
            tiled=True,
        ),
        lax.all_to_all(
            prompt_values.reshape(rows_here, prompt_count, ranks, head_width),
            "tensor",
            split_axis=2,
            concat_axis=0,
            tiled=True,
        ),
    )
    block_k = block_k.reshape(block_rows, prompt_count, head_width)
    block_v = block_v.reshape(block_rows, prompt_count, head_width)
    send_k = jnp.take(block_k, prompt_of, axis=1)
    send_v = jnp.take(block_v, prompt_of, axis=1)
    got_k, got_v = (
        lax.all_to_all(send_k, "dp", split_axis=1, concat_axis=0, tiled=True),
        lax.all_to_all(send_v, "dp", split_axis=1, concat_axis=0, tiled=True),
    )
    span_k = got_k.reshape(span_len, head_width)
    span_v = got_v.reshape(span_len, head_width)
    mixed, grad_q, grad_rkeys, grad_rvalues, grad_pkeys, grad_pvalues = attention(
        resp_queries, span_k, span_v, resp_keys, resp_values, out_grad, lengths
    )
    back_k, back_v = (
        lax.all_to_all(
            grad_pkeys.reshape(dp_count, block_rows, head_width),
            "dp",
            split_axis=0,
            concat_axis=0,
            tiled=True,
        ),
        lax.all_to_all(
            grad_pvalues.reshape(dp_count, block_rows, head_width),
            "dp",
            split_axis=0,
            concat_axis=0,
            tiled=True,
        ),
    )
    owners = (
        prompt_of[:, None] == lax.broadcasted_iota(jnp.int32, (dp_count, prompt_count), 1)
    ).astype(BF16)
    summed_k = jnp.einsum("sp,srw->rpw", owners, back_k, preferred_element_type=F32)
    summed_v = jnp.einsum("sp,srw->rpw", owners, back_v, preferred_element_type=F32)
    rows_k, rows_v = (
        lax.all_to_all(
            summed_k.astype(jnp.bfloat16).reshape(ranks, rows_here, prompt_count, 1, head_width),
            "tensor",
            split_axis=0,
            concat_axis=3,
            tiled=True,
        ),
        lax.all_to_all(
            summed_v.astype(jnp.bfloat16).reshape(ranks, rows_here, prompt_count, 1, head_width),
            "tensor",
            split_axis=0,
            concat_axis=3,
            tiled=True,
        ),
    )
    return (
        mixed,
        grad_q,
        grad_rkeys,
        grad_rvalues,
        rows_k.reshape(rows_here, prompt_count, ranks * head_width),
        rows_v.reshape(rows_here, prompt_count, ranks * head_width),
    )


def solution(mesh):
    return jax.shard_map(
        local,
        mesh=mesh,
        in_specs=(
            P("dp", "tensor"),
            P("dp", "tensor"),
            P("dp", "tensor"),
            P(("dp", "tensor"), None, None),
            P(("dp", "tensor"), None, None),
            P("dp", "tensor"),
            P("dp"),
            P(),
        ),
        out_specs=(
            P("dp", "tensor"),
            P("dp", "tensor"),
            P("dp", "tensor"),
            P("dp", "tensor"),
            P(("dp", "tensor"), None, None),
            P(("dp", "tensor"), None, None),
        ),
        check_vma=False,
    )
```

```python
import functools

import jax
import jax.numpy as jnp
from jax import lax
from jax.experimental import pallas as pl
from jax.experimental.pallas import tpu as pltpu
from jax.sharding import PartitionSpec as P

D = 128
F32 = jnp.float32
BF16 = jnp.bfloat16
SCALE = D ** -0.5
LOG2E = 1.4426950408889634
MESH = pl.DeviceIdType.MESH
PROMPTS = 4
RANKS = 8
Z, X, CORES = 4, 4, 2
PEERS = X * CORES
BLOCK = 128
CHUNK = PEERS * BLOCK
HALF = CHUNK // 2
TRF, TRB = 256, 512
X_ORDER = (2, 6, 3, 7, 4, 5, 1)


def dot_nt(a, b):
    return lax.dot_general(a, b, (((1,), (1,)), ((), ())), preferred_element_type=F32)


def dot_nn(a, b):
    return jnp.dot(a, b, preferred_element_type=F32)


def own_mask(len_ref, cols, resp_rows, dev_rows):
    key = lax.broadcasted_iota(jnp.int32, (dev_rows, cols), 0)
    row = lax.broadcasted_iota(jnp.int32, (dev_rows, cols), 1) % dev_rows
    length = jnp.where(key < resp_rows, len_ref[0], len_ref[1])
    return (key // resp_rows == row // resp_rows) & (key <= row) & (key % resp_rows < length)


def kernel(comm, owner_ref, len_ref, pin, q_ref, g_ref, rk_ref, rv_ref,
           o_ref, dq_ref, drk_ref, drv_ref, pout, *scratch):
    (zk, zv, xk, xv, ka, va, ts, t_own, qa, ga, m_s, mo_s, l_s, d_s, ot, vt, kt, acc_k, acc_v,
     gk, gv, rgk, rgv, sk, sv, rsk, rsv, sum_k, sum_v, bo_k, bo_v, back,
     t_send, t_recv, z_send, z_recv, x_send, x_recv,
     gx_send, gx_recv, gz_send, gz_recv, gt_send, gt_recv) = scratch
    rows = q_ref.shape[0]
    heads = q_ref.shape[1] // D
    half = rows // 2
    total = rows * heads

    dp, tensor = lax.axis_index("dp"), lax.axis_index("tensor")
    core, x_at, z_at = dp % CORES, dp // CORES % X, dp // (CORES * X)
    y_at, zl_at = tensor % 4, tensor // 4

    def dp_index(z, x, c):
        return (z * X + x) * CORES + c

    def x_peer(j, sign):
        return dp_index(z_at, (x_at + sign * (j // 2) + X) % X, (core + j) % CORES)

    def z_peer(d, sign):
        return dp_index((z_at + sign * d + Z) % Z, x_at, core)

    def t_peer(i):
        return (zl_at + i // 4) % 2 * 4 + (y_at + i) % 4

    def t_back(i):
        return (zl_at + i // 4) % 2 * 4 + (y_at - i % 4 + 4) % 4

    def remote(src, dst, send, recv, device):
        return pltpu.make_async_remote_copy(
            src_ref=src, dst_ref=dst, send_sem=send, recv_sem=recv, device_id=device, device_id_type=MESH)

    def rows_of(t):
        return pl.ds(pl.multiple_of(t * 16, 16), 16)

    owners = [owner_ref[x_peer(j, 1)] for j in range(PEERS)]

    def t_copy(i, kv):
        dst = (zk, zv)[kv][0]
        return remote(pin.at[t_peer(i), kv], dst.at[:, rows_of(tensor)],
                      t_send.at[2 * i + kv], t_recv.at[2 * i + kv], (dp, t_peer(i)))

    def z_copy(d, kv):
        ref = (zk, zv)[kv]
        return remote(ref[0], ref[d], z_send.at[2 * d + kv], z_recv.at[2 * d + kv], (z_peer(d, 1), tensor))

    def x_copy(d, kv, j):
        at = (d * 2 + kv) * PEERS + j
        return remote((xk, xv)[kv][d].at[j], (ka, va)[kv][d].at[pl.ds(j * BLOCK, BLOCK)],
                      x_send.at[at], x_recv.at[at], (x_peer(j, 1), tensor))

    def gx_copy(d, kv, j):
        at = (d * 2 + kv) * PEERS + j
        return remote((gk, gv)[kv][d].at[pl.ds(j * BLOCK, BLOCK)], (rgk, rgv)[kv][d].at[j],
                      gx_send.at[at], gx_recv.at[at], (x_peer(j, -1), tensor))

    def gz_copy(d, kv):
        return remote((sk, sv)[kv][d - 1], (rsk, rsv)[kv][d - 1],
                      gz_send.at[2 * d + kv], gz_recv.at[2 * d + kv], (z_peer(d, -1), tensor))

    def gt_copy(i, kv):
        return remote((bo_k, bo_v)[kv].at[:, rows_of(t_peer(i))], back.at[tensor, kv],
                      gt_send.at[2 * i + kv], gt_recv.at[2 * i + kv], (dp, t_peer(i)))

    def start(copies):
        if comm:
            for copy in copies:
                copy.start()

    def wait_recv(copies):
        if comm:
            for copy in copies:
                copy.wait_recv()

    def wait_send(copies):
        if comm:
            for copy in copies:
                copy.wait_send()

    if comm:
        barrier = pltpu.get_barrier_semaphore()
        for j in range(1, PEERS):
            pl.semaphore_signal(barrier, inc=1, device_id=(x_peer(j, -1), tensor), device_id_type=MESH)
        for d in range(1, Z):
            pl.semaphore_signal(barrier, inc=1, device_id=(z_peer(d, -1), tensor), device_id_type=MESH)
        for i in range(1, RANKS):
            pl.semaphore_signal(barrier, inc=1, device_id=(dp, t_back(i)), device_id_type=MESH)
        pl.semaphore_wait(barrier, PEERS - 1 + Z - 1 + RANKS - 1)

    t_all = [(i, kv) for kv in range(2) for i in range(1, RANKS)]
    start(t_copy(i, kv) for i, kv in t_all)
    for kv in range(2):
        (zk, zv)[kv][0][:, rows_of(tensor)] = pin[tensor, kv]

    row_ids = lax.broadcasted_iota(jnp.int32, (rows, D), 0)
    live = (row_ids % half) < jnp.where(row_ids < half, len_ref[0], len_ref[1])
    for h in range(heads):
        qa[h * rows:(h + 1) * rows] = q_ref[:, h * D:(h + 1) * D]
        g = g_ref[:, h * D:(h + 1) * D]
        ga[h * rows:(h + 1) * rows] = jnp.where(live, g, jnp.zeros_like(g))

    def select(d, kv):
        src, dst, own = (zk, zv)[kv][d], (xk, xv)[kv][d], (ka, va)[kv][d]
        own[0:BLOCK] = src[owners[0]]
        for j in X_ORDER:
            dst[j] = src[owners[j]]
            start([x_copy(d, kv, j)])

    def arrived(d, kv):
        wait_recv(x_copy(d, kv, j) for j in X_ORDER)

    def own_fwd():
        mask = own_mask(len_ref, TRF, half, rows)
        rvt = rv_ref[...].T

        def body(b, _):
            blk = pl.ds(pl.multiple_of(b * TRF, TRF), TRF)
            t = jnp.where(mask, dot_nt(rk_ref[...], qa[blk]) * (SCALE * LOG2E), -1e30)
            t_own[:, blk] = t
            m = jnp.max(t, axis=0, keepdims=True)
            e = jnp.exp2(t - m)
            m_s[:, blk] = m
            mo_s[:, blk] = m
            l_s[:, blk] = jnp.sum(e, axis=0, keepdims=True)
            ot[:, blk] = dot_nn(rvt, e.astype(BF16))
            return 0

        lax.fori_loop(0, total // TRF, body, 0)

    def score(d):
        def body(b, _):
            blk = pl.ds(pl.multiple_of(b * TRF, TRF), TRF)
            t = dot_nt(ka[d][...], qa[blk]) * (SCALE * LOG2E)
            ts[d][:, blk] = t
            m_s[:, blk] = jnp.maximum(m_s[:, blk], jnp.max(t, axis=0, keepdims=True))
            return 0

        lax.fori_loop(0, total // TRF, body, 0)

    def mix(d):
        vt[...] = va[d][...].T

        def body(b, _):
            blk = pl.ds(pl.multiple_of(b * TRF, TRF), TRF)
            m = m_s[:, blk]
            e = jnp.exp2(ts[d][:, blk] - m)
            alpha = jnp.exp2(mo_s[:, blk] - m)
            mo_s[:, blk] = m
            l_s[:, blk] = l_s[:, blk] * alpha + jnp.sum(e, axis=0, keepdims=True)
            ot[:, blk] = ot[:, blk] * alpha + dot_nn(vt[...], e.astype(BF16))
            return 0

        lax.fori_loop(0, total // TRF, body, 0)

    own_fwd()
    wait_recv(t_copy(i, 0) for i in range(1, RANKS))
    start([z_copy(1, 0), z_copy(3, 0)])
    select(0, 0)
    wait_recv(t_copy(i, 1) for i in range(1, RANKS))
    start([z_copy(1, 1), z_copy(3, 1)])
    select(0, 1)
    start([z_copy(2, 0), z_copy(2, 1)])
    arrived(0, 0)
    score(0)
    wait_recv([z_copy(1, 0)])
    select(1, 0)
    wait_recv([z_copy(3, 0)])
    select(3, 0)
    arrived(0, 1)
    mix(0)
    wait_recv([z_copy(1, 1)])
    select(1, 1)
    wait_recv([z_copy(3, 1)])
    select(3, 1)
    arrived(1, 0)
    score(1)
    arrived(3, 0)
    score(3)
    wait_recv([z_copy(2, 0)])
    select(2, 0)
    arrived(1, 1)
    mix(1)
    wait_recv([z_copy(2, 1)])
    select(2, 1)
    arrived(3, 1)
    mix(3)
    arrived(2, 0)
    score(2)
    arrived(2, 1)
    mix(2)

    for h in range(heads):
        blk = slice(h * rows, (h + 1) * rows)
        l = l_s[:, blk]
        o = ot[:, blk] / l
        d_s[:, blk] = jnp.sum(o * ga[blk].T.astype(F32), axis=0, keepdims=True)
        m_s[:, blk] = m_s[:, blk] + jnp.log2(l)
        o_ref[:, h * D:(h + 1) * D] = jnp.where(live, o.T, 0.0).astype(BF16)
    ot[...] = jnp.zeros_like(ot)

    def bwd_block(t, vs, kts, blk):
        qb, gb = qa[blk], ga[blk]
        p = jnp.exp2(t - m_s[:, blk])
        ds = (p * (dot_nt(vs, gb) - d_s[:, blk])).astype(BF16)
        dv = dot_nn(p.astype(BF16), gb)
        dk = dot_nn(ds, qb)
        ot[:, blk] += dot_nn(kts, ds)
        return dk, dv

    def bwd_half(d, part):
        at = slice(part * HALF, (part + 1) * HALF)
        kt[...] = ka[d][at].T
        acc_k[...] = jnp.zeros_like(acc_k)
        acc_v[...] = jnp.zeros_like(acc_v)

        def body(b, _):
            blk = pl.ds(pl.multiple_of(b * TRB, TRB), TRB)
            dk, dv = bwd_block(ts[d][at, blk], va[d][at], kt[...], blk)
            acc_k[...] += dk
            acc_v[...] += dv
            return 0

        lax.fori_loop(0, total // TRB, body, 0)
        gk[d][at] = (acc_k[...] * SCALE).astype(BF16)
        gv[d][at] = acc_v[...].astype(BF16)
        start(gx_copy(d, kv, j) for j in X_ORDER if j // (PEERS // 2) == part for kv in range(2))

    def own_bwd():
        rkt = rk_ref[...].T
        acc_k[:rows] = jnp.zeros((rows, D), F32)
        acc_v[:rows] = jnp.zeros((rows, D), F32)

        def body(b, _):
            blk = pl.ds(pl.multiple_of(b * TRB, TRB), TRB)
            dk, dv = bwd_block(t_own[:, blk], rv_ref[...], rkt, blk)
            acc_k[:rows] += dk
            acc_v[:rows] += dv
            return 0

        lax.fori_loop(0, total // TRB, body, 0)
        drk_ref[...] = (acc_k[:rows] * SCALE).astype(BF16)
        drv_ref[...] = acc_v[:rows].astype(BF16)

    picks = [[(owners[j] == p).astype(F32) for j in range(PEERS)] for p in range(PROMPTS)]

    def by_prompt(d, kv, at):
        mine, got = (gk, gv)[kv][d], (rgk, rgv)[kv][d]
        terms = [mine[at].astype(F32)] + [got[j, at].astype(F32) for j in range(1, PEERS)]
        sums = []
        for p in range(PROMPTS):
            value = terms[0] * picks[p][0]
            for j in range(1, PEERS):
                value = value + terms[j] * picks[p][j]
            sums.append(value)
        return sums

    def reduce(d):
        for kv in range(2):
            wait_recv(gx_copy(d, kv, j) for j in X_ORDER)

            def body(b, _):
                at = rows_of(b)
                for p, value in enumerate(by_prompt(d, kv, at)):
                    (sk, sv)[kv][d - 1][p, at] = value.astype(BF16)
                return 0

            lax.fori_loop(0, BLOCK // 16, body, 0)
            start([gz_copy(d, kv)])

    def reduce_own(kv):
        wait_recv(gx_copy(0, kv, j) for j in X_ORDER)

        def body(b, _):
            at = rows_of(b)
            for p, value in enumerate(by_prompt(0, kv, at)):
                (sum_k, sum_v)[kv][p, at] = value
            return 0

        lax.fori_loop(0, BLOCK // 16, body, 0)

    def gather_sums(kv):
        wait_recv(gz_copy(d, kv) for d in (2, 1, 3))
        got = (rsk, rsv)[kv]

        def body(b, _):
            at = rows_of(b)
            for p in range(PROMPTS):
                value = (sum_k, sum_v)[kv][p, at]
                for d in range(Z - 1):
                    value = value + got[d][p, at].astype(F32)
                (bo_k, bo_v)[kv][p, at] = value.astype(BF16)
            return 0

        lax.fori_loop(0, BLOCK // 16, body, 0)
        start(gt_copy(i, kv) for i in range(1, RANKS))
        back[tensor, kv] = (bo_k, bo_v)[kv][:, rows_of(tensor)]

    bwd_half(2, 0)
    bwd_half(2, 1)
    bwd_half(1, 0)
    reduce(2)
    bwd_half(1, 1)
    bwd_half(3, 0)
    reduce(1)
    bwd_half(3, 1)
    bwd_half(0, 0)
    reduce(3)
    bwd_half(0, 1)
    own_bwd()
    for h in range(heads):
        dq_ref[:, h * D:(h + 1) * D] = (ot[:, h * rows:(h + 1) * rows] * SCALE).T.astype(BF16)
    reduce_own(0)
    reduce_own(1)
    gather_sums(0)
    gather_sums(1)
    wait_recv(gt_copy(i, kv) for i, kv in t_all)
    pout[...] = back[...]

    wait_send(t_copy(i, kv) for i, kv in t_all)
    wait_send(z_copy(d, kv) for d in range(1, Z) for kv in range(2))
    wait_send(x_copy(d, kv, j) for d in range(Z) for kv in range(2) for j in X_ORDER)
    wait_send(gx_copy(d, kv, j) for d in range(Z) for kv in range(2) for j in X_ORDER)
    wait_send(gz_copy(d, kv) for d in range(1, Z) for kv in range(2))
    wait_send(gt_copy(i, kv) for i, kv in t_all)


def attention(owner, lengths, pin, q, g, rk, rv, comm=True):
    rows, width = q.shape
    total = rows * width // D
    vm = pl.BlockSpec(memory_space=pltpu.VMEM)
    sm = pl.BlockSpec(memory_space=pltpu.SMEM)
    vmem = pltpu.VMEM
    dma = pltpu.SemaphoreType.DMA

    def some(count, shape, dtype=BF16):
        return [vmem(shape, dtype) for _ in range(count)]

    prompts = (PROMPTS, BLOCK, D)
    scratch = [
        some(Z, prompts), some(Z, prompts),
        some(Z, (PEERS, BLOCK, D)), some(Z, (PEERS, BLOCK, D)),
        some(Z, (CHUNK, D)), some(Z, (CHUNK, D)),
        some(Z, (CHUNK, total), F32), vmem((rows, total), F32),
        vmem((total, D), BF16), vmem((total, D), BF16),
        vmem((1, total), F32), vmem((1, total), F32), vmem((1, total), F32), vmem((1, total), F32),
        vmem((D, total), F32), vmem((D, CHUNK), BF16), vmem((D, HALF), BF16),
        vmem((HALF, D), F32), vmem((HALF, D), F32),
        some(Z, (CHUNK, D)), some(Z, (CHUNK, D)),
        some(Z, (PEERS, BLOCK, D)), some(Z, (PEERS, BLOCK, D)),
        some(Z - 1, prompts), some(Z - 1, prompts), some(Z - 1, prompts), some(Z - 1, prompts),
        vmem(prompts, F32), vmem(prompts, F32), vmem(prompts, BF16), vmem(prompts, BF16),
        vmem((RANKS, 2, PROMPTS, 16, D), BF16),
        dma((2 * RANKS,)), dma((2 * RANKS,)), dma((2 * Z,)), dma((2 * Z,)),
        dma((2 * Z * PEERS,)), dma((2 * Z * PEERS,)), dma((2 * Z * PEERS,)), dma((2 * Z * PEERS,)),
        dma((2 * Z,)), dma((2 * Z,)), dma((2 * RANKS,)), dma((2 * RANKS,)),
    ]
    extra = dict(collective_id=0, has_side_effects=True) if comm else {}
    return pl.pallas_call(
        functools.partial(kernel, comm),
        out_shape=(
            jax.ShapeDtypeStruct(q.shape, BF16),
            jax.ShapeDtypeStruct(q.shape, BF16),
            jax.ShapeDtypeStruct(rk.shape, BF16),
            jax.ShapeDtypeStruct(rk.shape, BF16),
            jax.ShapeDtypeStruct(pin.shape, BF16),
        ),
        in_specs=[sm, sm] + [vm] * 5,
        out_specs=(vm,) * 5,
        scratch_shapes=scratch,
        compiler_params=pltpu.CompilerParams(vmem_limit_bytes=62 * 2 ** 20, **extra),
    )(owner, lengths, pin, q, g, rk, rv)


def local(q, rk, rv, prompt_keys, prompt_values, g, lengths, prompt_of):
    rows_here, prompts, width = prompt_keys.shape
    both = jnp.stack([prompt_keys, prompt_values]).reshape(2, rows_here, prompts, RANKS, D)
    pin = jnp.transpose(both, (3, 0, 2, 1, 4))
    o, dq, drk, drv, back = attention(prompt_of, lengths, pin, q, g, rk, rv)
    back = jnp.transpose(back, (1, 3, 2, 0, 4)).reshape(2, rows_here, prompts, width)
    return o, dq, drk, drv, back[0], back[1]


def solution(mesh):
    heads = P("dp", "tensor")
    prompt = P(("dp", "tensor"), None, None)
    return jax.shard_map(
        local,
        mesh=mesh,
        in_specs=(heads, heads, heads, prompt, prompt, heads, P("dp"), P()),
        out_specs=(heads, heads, heads, heads, prompt, prompt),
        check_vma=False,
    )
```

```python
import functools

import jax
import jax.numpy as jnp
from jax import lax
from jax.experimental import pallas as pl
from jax.experimental.pallas import tpu as pltpu
from jax.sharding import PartitionSpec as P

D = 128
F32 = jnp.float32
BF16 = jnp.bfloat16
SCALE = D ** -0.5
LOG2E = 1.4426950408889634
MESH = pl.DeviceIdType.MESH
PROMPTS = 4
RANKS = 8
Z, X, CORES = 4, 4, 2
PEERS = X * CORES
PARTS = 2
BLOCK = 64
UNIT = PEERS * BLOCK
TRF, TRB = 1024, 1024
X_ORDER = (2, 6, 3, 7, 4, 5, 1)


def dot_nt(a, b):
    return lax.dot_general(a, b, (((1,), (1,)), ((), ())), preferred_element_type=F32)


def dot_nn(a, b):
    return jnp.dot(a, b, preferred_element_type=F32)


def own_mask(len_ref, cols, resp_rows, dev_rows):
    key = lax.broadcasted_iota(jnp.int32, (dev_rows, cols), 0)
    row = lax.broadcasted_iota(jnp.int32, (dev_rows, cols), 1) % dev_rows
    length = jnp.where(key < resp_rows, len_ref[0], len_ref[1])
    return (key // resp_rows == row // resp_rows) & (key <= row) & (key % resp_rows < length)


def kernel(comm, owner_ref, len_ref, pk_hbm, pv_hbm, q_hbm, g_hbm, rk_hbm, rv_hbm,
           o_hbm, dq_hbm, drk_hbm, drv_hbm, pko_hbm, pvo_hbm, *scratch):
    (pk, pv, q_in, g_in, rk, rv, o_out, dq_out, drk, drv, pin, back,
     own_zk, own_zv, zk, zv, xk, xv, ka, va, ts, t_own, qa, ga, gat, m_s, mo_s, l_s, d_s, ot, dqt, vt, kt,
     acc_k, acc_v, gu, rgu, su, rsu, relay, own_sum, bo,
     io, t_send, t_recv, z_send, z_recv, x_send, x_recv,
     gx_send, gx_recv, gz_send, gz_recv, gt_send, gt_recv) = scratch
    rows, width = q_in.shape
    heads = width // D
    half = rows // 2
    total = rows * heads

    dp, tensor = lax.axis_index("dp"), lax.axis_index("tensor")
    core, x_at, z_at = dp % CORES, dp // CORES % X, dp // (CORES * X)
    y_at, zl_at = tensor % 4, tensor // 4

    def dp_index(z, x, c):
        return (z * X + x) * CORES + c

    def x_peer(j, sign):
        return dp_index(z_at, (x_at + sign * (j // 2) + X) % X, (core + j) % CORES)

    def z_peer(step):
        return dp_index((z_at + step + Z) % Z, x_at, core)

    def t_peer(i):
        return (zl_at + i // 4) % 2 * 4 + (y_at + i) % 4

    def t_back(i):
        return (zl_at + i // 4) % 2 * 4 + (y_at - i % 4 + 4) % 4

    def remote(src, dst, send, recv, device):
        return pltpu.make_async_remote_copy(
            src_ref=src, dst_ref=dst, send_sem=send, recv_sem=recv, device_id=device, device_id_type=MESH)

    def rows_of(t):
        return pl.ds(pl.multiple_of(t * 16, 16), 16)

    owners = [owner_ref[x_peer(j, 1)] for j in range(PEERS)]

    def t_copy(i, kv):
        dst = (own_zk, own_zv)[kv]
        return remote(pin.at[t_peer(i), kv], dst.at[tensor // 4, :, rows_of(tensor % 4)],
                      t_send.at[2 * i + kv], t_recv.at[2 * i + kv], (dp, t_peer(i)))

    def z_block(d, r, kv):
        return (own_zk, own_zv)[kv].at[r] if d == 0 else (zk, zv)[kv][2 * d + r]

    def z_copy(d, r, kv):
        at = (d * 2 + r) * 2 + kv
        src = z_block(0, r, kv) if d != 2 else z_block((1, 3)[r], r, kv)
        step = {1: 1, 3: -1, 2: (1, -1)[r]}[d]
        return remote(src, z_block(d, r, kv), z_send.at[at], z_recv.at[at], (z_peer(step), tensor))

    def x_copy(d, r, kv, j):
        u = 2 * d + r
        at = (u * 2 + kv) * PEERS + j
        return remote((xk, xv)[kv][u].at[j], (ka, va)[kv][u].at[pl.ds(j * BLOCK, BLOCK)],
                      x_send.at[at], x_recv.at[at], (x_peer(j, 1), tensor))

    def gx_copy(d, r, j):
        u = 2 * d + r
        at = u * PEERS + j
        return remote(gu[u].at[j], rgu[u].at[j], gx_send.at[at], gx_recv.at[at], (x_peer(j, -1), tensor))

    def gz_copy(d, r):
        u = 2 * d + r
        dst = relay[r] if d == 2 else rsu[u]
        step = {1: -1, 3: 1, 2: (-1, 1)[r]}[d]
        return remote(su[u], dst, gz_send.at[u], gz_recv.at[u], (z_peer(step), tensor))

    def gt_copy(i):
        to = t_peer(i)
        return remote(bo.at[to // 4, :, :, rows_of(to % 4)], back.at[tensor],
                      gt_send.at[i], gt_recv.at[i], (dp, to))

    def start(copies):
        if comm:
            for copy in copies:
                copy.start()

    def wait_recv(copies):
        if comm:
            for copy in copies:
                copy.wait_recv()

    def wait_send(copies):
        if comm:
            for copy in copies:
                copy.wait_send()

    loads = [pltpu.make_async_copy(src, dst, io.at[n]) for n, (src, dst) in enumerate(
        [(pk_hbm, pk), (pv_hbm, pv), (q_hbm, q_in), (g_hbm, g_in), (rk_hbm, rk), (rv_hbm, rv)])]
    stores = [pltpu.make_async_copy(src, dst, io.at[6 + n]) for n, (src, dst) in enumerate(
        [(o_out, o_hbm), (dq_out, dq_hbm), (drk, drk_hbm), (drv, drv_hbm), (pk, pko_hbm), (pv, pvo_hbm)])]
    for copy in loads:
        copy.start()

    if comm:
        barrier = pltpu.get_barrier_semaphore()
        for j in range(1, PEERS):
            pl.semaphore_signal(barrier, inc=1, device_id=(x_peer(j, -1), tensor), device_id_type=MESH)
        for step in (1, -1):
            pl.semaphore_signal(barrier, inc=1, device_id=(z_peer(step), tensor), device_id_type=MESH)
        for i in range(1, RANKS):
            pl.semaphore_signal(barrier, inc=1, device_id=(dp, t_back(i)), device_id_type=MESH)

    for kv in range(2):
        loads[kv].wait()
        for t in range(RANKS):
            for p in range(PROMPTS):
                at = p * RANKS * D + t * D
                pin[t, kv, p] = (pk, pv)[kv][:, at:at + D]
    if comm:
        pl.semaphore_wait(barrier, PEERS - 1 + 2 + RANKS - 1)

    t_all = [(i, kv) for kv in range(2) for i in range(1, RANKS)]
    start(t_copy(i, kv) for i, kv in t_all)
    for kv in range(2):
        (own_zk, own_zv)[kv][tensor // 4, :, rows_of(tensor % 4)] = pin[tensor, kv]
    for copy in loads[2:]:
        copy.wait()

    row_ids = lax.broadcasted_iota(jnp.int32, (rows, D), 0)
    live = (row_ids % half) < jnp.where(row_ids < half, len_ref[0], len_ref[1])
    for h in range(heads):
        qa[h * rows:(h + 1) * rows] = q_in[:, h * D:(h + 1) * D]
        g = g_in[:, h * D:(h + 1) * D]
        ga[h * rows:(h + 1) * rows] = jnp.where(live, g, jnp.zeros_like(g))

    def select(d, r, kv):
        u = 2 * d + r
        src, dst, own = z_block(d, r, kv), (xk, xv)[kv][u], (ka, va)[kv][u]
        own[0:BLOCK] = src[owners[0]]
        for j in X_ORDER:
            dst[j] = src[owners[j]]
            start([x_copy(d, r, kv, j)])

    def arrived(d, r, kv):
        wait_recv(x_copy(d, r, kv, j) for j in X_ORDER)

    def by_rows(size, body):
        def step(b, _):
            body(pl.ds(pl.multiple_of(b * size, size), size))
            return 0

        lax.fori_loop(0, total // size, step, 0)

    def own_fwd():
        mask = own_mask(len_ref, TRF, half, rows)
        rvt = rv[...].T

        def body(blk):
            t = jnp.where(mask, dot_nt(rk[...], qa[blk]) * (SCALE * LOG2E), -1e30)
            t_own[:, blk] = t
            m = jnp.max(t, axis=0, keepdims=True)
            e = jnp.exp2(t - m)
            m_s[:, blk] = m
            mo_s[:, blk] = m
            l_s[:, blk] = jnp.sum(e, axis=0, keepdims=True)
            ot[:, blk] = dot_nn(rvt, e.astype(BF16))

        by_rows(TRF, body)

    def turn_grads():
        for h in range(heads):
            at = slice(h * rows, (h + 1) * rows)
            gat[:, at] = ga[at].T

    def score(d, r):
        u = 2 * d + r
        arrived(d, r, 0)

        def body(blk):
            t = dot_nt(ka[u][...], qa[blk]) * (SCALE * LOG2E)
            ts[u][:, blk] = t
            m_s[:, blk] = jnp.maximum(m_s[:, blk], jnp.max(t, axis=0, keepdims=True))

        by_rows(TRF, body)

    def mix(d, r):
        u = 2 * d + r
        arrived(d, r, 1)
        vt[...] = va[u][...].T

        def body(blk):
            m = m_s[:, blk]
            e = jnp.exp2(ts[u][:, blk] - m)
            alpha = jnp.exp2(mo_s[:, blk] - m)
            mo_s[:, blk] = m
            l_s[:, blk] = l_s[:, blk] * alpha + jnp.sum(e, axis=0, keepdims=True)
            ot[:, blk] = ot[:, blk] * alpha + dot_nn(vt[...], e.astype(BF16))

        by_rows(TRF, body)

    def z_in(items):
        wait_recv(z_copy(*item) for item in items)

    wait_recv(t_copy(i, 0) for i in range(1, RANKS))
    start(z_copy(d, r, 0) for r in (0, 1) for d in (1, 3))
    select(0, 0, 0)
    select(0, 1, 0)
    wait_recv(t_copy(i, 1) for i in range(1, RANKS))
    select(0, 0, 1)
    select(0, 1, 1)
    own_fwd()
    score(0, 0)
    z_in([(1, 0, 0), (3, 0, 0)])
    start([z_copy(1, 0, 1), z_copy(3, 0, 1)])
    select(1, 0, 0)
    select(3, 0, 0)
    score(0, 1)
    mix(0, 0)
    z_in([(1, 1, 0), (3, 1, 0)])
    start([z_copy(1, 1, 1), z_copy(3, 1, 1)])
    select(1, 1, 0)
    select(3, 1, 0)
    mix(0, 1)
    turn_grads()
    score(1, 0)
    z_in([(1, 0, 1), (3, 0, 1)])
    start([z_copy(2, 0, 0), z_copy(2, 1, 0)])
    select(1, 0, 1)
    select(3, 0, 1)
    score(3, 0)
    score(1, 1)
    z_in([(1, 1, 1), (3, 1, 1)])
    start([z_copy(2, 0, 1), z_copy(2, 1, 1)])
    select(1, 1, 1)
    select(3, 1, 1)
    score(3, 1)
    mix(1, 0)
    z_in([(2, 0, 0), (2, 1, 0)])
    select(2, 0, 0)
    select(2, 1, 0)
    mix(3, 0)
    mix(1, 1)
    z_in([(2, 0, 1), (2, 1, 1)])
    select(2, 0, 1)
    select(2, 1, 1)
    mix(3, 1)
    score(2, 0)
    score(2, 1)
    mix(2, 0)
    mix(2, 1)

    def stats(blk):
        l = l_s[:, blk]
        o = ot[:, blk] / l
        ot[:, blk] = o
        d_s[:, blk] = jnp.sum(o * gat[:, blk].astype(F32), axis=0, keepdims=True)
        m_s[:, blk] = m_s[:, blk] + jnp.log2(l)
        dqt[:, blk] = jnp.zeros((D, TRF), F32)

    by_rows(TRF, stats)

    def write_out():
        for h in range(heads):
            o = ot[:, h * rows:(h + 1) * rows].T
            o_out[:, h * D:(h + 1) * D] = jnp.where(live, o, 0.0).astype(BF16)
        stores[0].start()

    def bwd_block(t, vs, kts, blk):
        qb, gb = qa[blk], ga[blk]
        p = jnp.exp2(t - m_s[:, blk])
        ds = (p * (dot_nt(vs, gb) - d_s[:, blk])).astype(BF16)
        dv = dot_nn(p.astype(BF16), gb)
        dk = dot_nn(ds, qb)
        dqt[:, blk] += dot_nn(kts, ds)
        return dk, dv

    def bwd(d, r):
        u = 2 * d + r
        kt[...] = ka[u][...].T
        acc_k[...] = jnp.zeros_like(acc_k)
        acc_v[...] = jnp.zeros_like(acc_v)

        def body(blk):
            dk, dv = bwd_block(ts[u][:, blk], va[u][...], kt[...], blk)
            acc_k[...] += dk
            acc_v[...] += dv

        by_rows(TRB, body)
        gu[u][:, 0] = (acc_k[...] * SCALE).astype(BF16).reshape(PEERS, BLOCK, D)
        gu[u][:, 1] = acc_v[...].astype(BF16).reshape(PEERS, BLOCK, D)
        start(gx_copy(d, r, j) for j in X_ORDER)

    def own_bwd():
        rkt = rk[...].T
        acc_k[:rows] = jnp.zeros((rows, D), F32)
        acc_v[:rows] = jnp.zeros((rows, D), F32)

        def body(blk):
            dk, dv = bwd_block(t_own[:, blk], rv[...], rkt, blk)
            acc_k[:rows] += dk
            acc_v[:rows] += dv

        by_rows(TRB, body)
        drk[...] = (acc_k[:rows] * SCALE).astype(BF16)
        drv[...] = acc_v[:rows].astype(BF16)
        for h in range(heads):
            dq_out[:, h * D:(h + 1) * D] = (dqt[:, h * rows:(h + 1) * rows] * SCALE).T.astype(BF16)
        for copy in stores[1:4]:
            copy.start()

    picks = [[(owners[j] == p).astype(F32) for j in range(PEERS)] for p in range(PROMPTS)]

    def reduce(d, r):
        u = 2 * d + r
        wait_recv(gx_copy(d, r, j) for j in X_ORDER)
        passing = (d, r) in ((1, 0), (3, 1))
        if passing:
            wait_recv([gz_copy(2, r)])

        def body(b, _):
            at = rows_of(b)
            for kv in range(2):
                terms = [gu[u][0, kv, at].astype(F32)] + [rgu[u][j, kv, at].astype(F32) for j in range(1, PEERS)]
                for p in range(PROMPTS):
                    value = terms[0] * picks[p][0]
                    for j in range(1, PEERS):
                        value = value + terms[j] * picks[p][j]
                    if passing:
                        value = value + relay[r][kv, p, at].astype(F32)
                    if d == 0:
                        own_sum[r][kv, p, at] = value
                    else:
                        su[u][kv, p, at] = value.astype(BF16)
            return 0

        lax.fori_loop(0, BLOCK // 16, body, 0)
        if d:
            start([gz_copy(d, r)])

    def finish(r):
        wait_recv(gz_copy(d, r) for d in (1, 3))

        def body(b, _):
            at = rows_of(b)
            for kv in range(2):
                for p in range(PROMPTS):
                    value = own_sum[r][kv, p, at]
                    for d in (1, 3):
                        value = value + rsu[2 * d + r][kv, p, at].astype(F32)
                    bo[r, kv, p, at] = value.astype(BF16)
            return 0

        lax.fori_loop(0, BLOCK // 16, body, 0)

    bwd(2, 0)
    bwd(2, 1)
    bwd(1, 1)
    reduce(2, 0)
    bwd(3, 0)
    reduce(2, 1)
    bwd(1, 0)
    write_out()
    reduce(1, 1)
    bwd(3, 1)
    reduce(3, 0)
    bwd(0, 0)
    reduce(1, 0)
    bwd(0, 1)
    reduce(3, 1)
    own_bwd()
    reduce(0, 0)
    finish(0)
    reduce(0, 1)
    finish(1)
    start(gt_copy(i) for i in range(1, RANKS))
    back[tensor] = bo[tensor // 4, :, :, rows_of(tensor % 4)]

    wait_send(t_copy(i, kv) for i, kv in t_all)
    wait_send(z_copy(d, r, kv) for d in range(1, Z) for r in range(2) for kv in range(2))
    wait_send(x_copy(d, r, kv, j) for d in range(Z) for r in range(2) for kv in range(2) for j in X_ORDER)
    wait_send(gx_copy(d, r, j) for d in range(Z) for r in range(2) for j in X_ORDER)
    wait_send(gz_copy(d, r) for d in range(1, Z) for r in range(2))

    wait_recv(gt_copy(i) for i in range(1, RANKS))
    for kv in range(2):
        for t in range(RANKS):
            for p in range(PROMPTS):
                at = p * RANKS * D + t * D
                (pk, pv)[kv][:, at:at + D] = back[t, kv, p]
        stores[4 + kv].start()
    wait_send(gt_copy(i) for i in range(1, RANKS))
    for copy in stores:
        copy.wait()


def attention(owner, lengths, pk, pv, q, g, rk, rv, comm=True):
    rows, width = q.shape
    total = rows * width // D
    hbm = pl.BlockSpec(memory_space=pl.ANY)
    sm = pl.BlockSpec(memory_space=pltpu.SMEM)
    vmem = pltpu.VMEM
    dma = pltpu.SemaphoreType.DMA
    units = Z * PARTS

    def some(count, shape, dtype=BF16):
        return [vmem(shape, dtype) for _ in range(count)]

    block = (PROMPTS, BLOCK, D)
    scratch = [
        vmem(pk.shape, BF16), vmem(pv.shape, BF16), vmem(q.shape, BF16), vmem(q.shape, BF16),
        vmem(rk.shape, BF16), vmem(rk.shape, BF16), vmem(q.shape, BF16), vmem(q.shape, BF16),
        vmem(rk.shape, BF16), vmem(rk.shape, BF16),
        vmem((RANKS, 2, PROMPTS, 16, D), BF16), vmem((RANKS, 2, PROMPTS, 16, D), BF16),
        vmem((PARTS, *block), BF16), vmem((PARTS, *block), BF16), some(units, block), some(units, block),
        some(units, (PEERS, BLOCK, D)), some(units, (PEERS, BLOCK, D)),
        some(units, (UNIT, D)), some(units, (UNIT, D)),
        some(units, (UNIT, total), F32), vmem((rows, total), F32),
        vmem((total, D), BF16), vmem((total, D), BF16), vmem((D, total), BF16),
        vmem((1, total), F32), vmem((1, total), F32), vmem((1, total), F32), vmem((1, total), F32),
        vmem((D, total), F32), vmem((D, total), F32), vmem((D, UNIT), BF16), vmem((D, UNIT), BF16),
        vmem((UNIT, D), F32), vmem((UNIT, D), F32),
        some(units, (PEERS, 2, BLOCK, D)), some(units, (PEERS, 2, BLOCK, D)),
        some(units, (2, *block)), some(units, (2, *block)), some(PARTS, (2, *block)),
        some(PARTS, (2, *block), F32), vmem((PARTS, 2, *block), BF16),
        dma((12,)), dma((2 * RANKS,)), dma((2 * RANKS,)), dma((2 * units,)), dma((2 * units,)),
        dma((2 * units * PEERS,)), dma((2 * units * PEERS,)), dma((units * PEERS,)), dma((units * PEERS,)),
        dma((units,)), dma((units,)), dma((RANKS,)), dma((RANKS,)),
    ]
    extra = dict(collective_id=0, has_side_effects=True) if comm else {}
    return pl.pallas_call(
        functools.partial(kernel, comm),
        out_shape=(
            jax.ShapeDtypeStruct(q.shape, BF16),
            jax.ShapeDtypeStruct(q.shape, BF16),
            jax.ShapeDtypeStruct(rk.shape, BF16),
            jax.ShapeDtypeStruct(rk.shape, BF16),
            jax.ShapeDtypeStruct(pk.shape, BF16),
            jax.ShapeDtypeStruct(pv.shape, BF16),
        ),
        in_specs=[sm, sm] + [hbm] * 6,
        out_specs=(hbm,) * 6,
        scratch_shapes=scratch,
        compiler_params=pltpu.CompilerParams(vmem_limit_bytes=62 * 2 ** 20, **extra),
    )(owner, lengths, pk, pv, q, g, rk, rv)


def local(q, rk, rv, prompt_keys, prompt_values, g, lengths, prompt_of):
    shape = prompt_keys.shape
    flat = (shape[0], shape[1] * shape[2])
    o, dq, drk, drv, dpk, dpv = attention(
        prompt_of, lengths, prompt_keys.reshape(flat), prompt_values.reshape(flat), q, g, rk, rv
    )
    return o, dq, drk, drv, dpk.reshape(shape), dpv.reshape(shape)


def solution(mesh):
    heads = P("dp", "tensor")
    prompt = P(("dp", "tensor"), None, None)
    return jax.shard_map(
        local,
        mesh=mesh,
        in_specs=(heads, heads, heads, prompt, prompt, heads, P("dp"), P()),
        out_specs=(heads, heads, heads, heads, prompt, prompt),
        check_vma=False,
    )
```

```python
import functools

import jax
import jax.numpy as jnp
from jax import lax
from jax.experimental import pallas as pl
from jax.experimental.pallas import tpu as pltpu
from jax.sharding import PartitionSpec as P

D = 128
F32 = jnp.float32
BF16 = jnp.bfloat16
SCALE = D ** -0.5
LOG2E = 1.4426950408889634
MESH = pl.DeviceIdType.MESH
PROMPTS = 4
RANKS = 8
Z, X, CORES = 4, 4, 2
PEERS = X * CORES
PARTS = 2
BLOCK = 64
UNIT = PEERS * BLOCK
TRF, TRB = 1024, 2048
X_ORDER = (4, 5, 2, 6, 3, 7, 1)


def dot_nt(a, b):
    return lax.dot_general(a, b, (((1,), (1,)), ((), ())), preferred_element_type=F32)


def dot_nn(a, b):
    return jnp.dot(a, b, preferred_element_type=F32)


def own_mask(len_ref, cols, resp_rows, dev_rows):
    key = lax.broadcasted_iota(jnp.int32, (dev_rows, cols), 0)
    row = lax.broadcasted_iota(jnp.int32, (dev_rows, cols), 1) % dev_rows
    length = jnp.where(key < resp_rows, len_ref[0], len_ref[1])
    return (key // resp_rows == row // resp_rows) & (key <= row) & (key % resp_rows < length)


def kernel(comm, owner_ref, len_ref, pk_hbm, pv_hbm, q_hbm, g_hbm, rk_hbm, rv_hbm,
           o_hbm, dq_hbm, drk_hbm, drv_hbm, pko_hbm, pvo_hbm, *scratch):
    (pk, pv, q_in, g_in, rk, rv, o_out, dq_out, drk, drv, pin, back,
     own_zk, own_zv, zk, zv, xk, xv, ka, va, ts, t_own, qa, ga, gat, m_s, mo_s, l_s, d_s, ot, dqt, vt, kt,
     acc_k, acc_v, gu, rgu, su, rsu, relay, own_sum, bo,
     io, t_send, t_recv, z_send, z_recv, x_send, x_recv,
     gx_send, gx_recv, gz_send, gz_recv, gt_send, gt_recv) = scratch
    rows, width = q_in.shape
    heads = width // D
    half = rows // 2
    total = rows * heads

    dp, tensor = lax.axis_index("dp"), lax.axis_index("tensor")
    core, x_at, z_at = dp % CORES, dp // CORES % X, dp // (CORES * X)
    y_at, zl_at = tensor % 4, tensor // 4

    def dp_index(z, x, c):
        return (z * X + x) * CORES + c

    def x_peer(j, sign):
        return dp_index(z_at, (x_at + sign * (j // 2) + X) % X, (core + j) % CORES)

    def z_peer(step):
        return dp_index((z_at + step + Z) % Z, x_at, core)

    def t_peer(i):
        return (zl_at + i // 4) % 2 * 4 + (y_at + i) % 4

    def t_back(i):
        return (zl_at + i // 4) % 2 * 4 + (y_at - i % 4 + 4) % 4

    def remote(src, dst, send, recv, device):
        return pltpu.make_async_remote_copy(
            src_ref=src, dst_ref=dst, send_sem=send, recv_sem=recv, device_id=device, device_id_type=MESH)

    def rows_of(t):
        return pl.ds(pl.multiple_of(t * 16, 16), 16)

    owners = [owner_ref[x_peer(j, 1)] for j in range(PEERS)]

    def t_copy(i, kv):
        dst = (own_zk, own_zv)[kv]
        return remote(pin.at[t_peer(i), kv], dst.at[tensor // 4, :, rows_of(tensor % 4)],
                      t_send.at[2 * i + kv], t_recv.at[2 * i + kv], (dp, t_peer(i)))

    def z_block(d, r, kv):
        return (own_zk, own_zv)[kv].at[r] if d == 0 else (zk, zv)[kv][2 * d + r]

    def z_copy(d, r, kv):
        at = (d * 2 + r) * 2 + kv
        src = z_block(0, r, kv) if d != 2 else z_block((1, 3)[r], r, kv)
        step = {1: 1, 3: -1, 2: (1, -1)[r]}[d]
        return remote(src, z_block(d, r, kv), z_send.at[at], z_recv.at[at], (z_peer(step), tensor))

    def x_copy(d, r, kv, j):
        u = 2 * d + r
        at = (u * 2 + kv) * PEERS + j
        return remote((xk, xv)[kv][u].at[j], (ka, va)[kv][u].at[pl.ds(j * BLOCK, BLOCK)],
                      x_send.at[at], x_recv.at[at], (x_peer(j, 1), tensor))

    def gx_copy(d, r, j):
        u = 2 * d + r
        at = u * PEERS + j
        return remote(gu[u].at[j], rgu[u].at[j], gx_send.at[at], gx_recv.at[at], (x_peer(j, -1), tensor))

    def gz_copy(d, r):
        u = 2 * d + r
        dst = relay[r] if d == 2 else rsu[u]
        step = {1: -1, 3: 1, 2: (-1, 1)[r]}[d]
        return remote(su[u], dst, gz_send.at[u], gz_recv.at[u], (z_peer(step), tensor))

    def gt_copy(r, k):
        to_y = (y_at + k) % 4
        at = (r + 2 - zl_at) % 2 * 4 + k
        return remote(bo.at[r, :, :, rows_of(to_y)], back.at[tensor],
                      gt_send.at[at], gt_recv.at[at], (dp, r * 4 + to_y))

    def start(copies):
        if comm:
            for copy in copies:
                copy.start()

    def wait_recv(copies):
        if comm:
            for copy in copies:
                copy.wait_recv()

    def wait_send(copies):
        if comm:
            for copy in copies:
                copy.wait_send()

    loads = [pltpu.make_async_copy(src, dst, io.at[n]) for n, (src, dst) in enumerate(
        [(pk_hbm, pk), (pv_hbm, pv), (q_hbm, q_in), (g_hbm, g_in), (rk_hbm, rk), (rv_hbm, rv)])]
    stores = [pltpu.make_async_copy(src, dst, io.at[6 + n]) for n, (src, dst) in enumerate(
        [(o_out, o_hbm), (dq_out, dq_hbm), (drk, drk_hbm), (drv, drv_hbm), (pk, pko_hbm), (pv, pvo_hbm)])]
    for copy in loads:
        copy.start()

    if comm:
        barrier = pltpu.get_barrier_semaphore()
        for j in range(1, PEERS):
            pl.semaphore_signal(barrier, inc=1, device_id=(x_peer(j, -1), tensor), device_id_type=MESH)
        for step in (1, -1):
            pl.semaphore_signal(barrier, inc=1, device_id=(z_peer(step), tensor), device_id_type=MESH)
        for i in range(1, RANKS):
            pl.semaphore_signal(barrier, inc=1, device_id=(dp, t_back(i)), device_id_type=MESH)

    t_all = [(i, kv) for kv in range(2) for i in range(1, RANKS)]
    for kv in range(2):
        loads[kv].wait()
        for t in range(RANKS):
            pin[t, kv] = jnp.swapaxes((pk, pv)[kv][:, :, t * D:(t + 1) * D], 0, 1)
        if comm and kv == 0:
            pl.semaphore_wait(barrier, PEERS - 1 + 2 + RANKS - 1)
        start(t_copy(i, kv) for i in range(1, RANKS))
    for kv in range(2):
        (own_zk, own_zv)[kv][tensor // 4, :, rows_of(tensor % 4)] = pin[tensor, kv]
    for copy in loads[2:]:
        copy.wait()

    row_ids = lax.broadcasted_iota(jnp.int32, (rows, D), 0)
    live = (row_ids % half) < jnp.where(row_ids < half, len_ref[0], len_ref[1])
    for h in range(heads):
        qa[h * rows:(h + 1) * rows] = q_in[:, h * D:(h + 1) * D]
        g = g_in[:, h * D:(h + 1) * D]
        ga[h * rows:(h + 1) * rows] = jnp.where(live, g, jnp.zeros_like(g))

    def select(d, r, kv):
        u = 2 * d + r
        src, dst, own = z_block(d, r, kv), (xk, xv)[kv][u], (ka, va)[kv][u]
        own[0:BLOCK] = src[owners[0]]
        for j in X_ORDER:
            dst[j] = src[owners[j]]
            start([x_copy(d, r, kv, j)])

    def arrived(d, r, kv):
        wait_recv(x_copy(d, r, kv, j) for j in X_ORDER)

    def by_rows(size, body):
        def step(b, _):
            body(pl.ds(pl.multiple_of(b * size, size), size))
            return 0

        lax.fori_loop(0, total // size, step, 0)

    def own_fwd():
        mask = own_mask(len_ref, TRF, half, rows)
        rvt = rv[...].T

        def body(blk):
            t = jnp.where(mask, dot_nt(rk[...], qa[blk]) * (SCALE * LOG2E), -1e30)
            t_own[:, blk] = t
            m = jnp.max(t, axis=0, keepdims=True)
            e = jnp.exp2(t - m)
            m_s[:, blk] = m
            mo_s[:, blk] = m
            l_s[:, blk] = jnp.sum(e, axis=0, keepdims=True)
            ot[:, blk] = dot_nn(rvt, e.astype(BF16))

        by_rows(TRF, body)

    def turn_grads():
        for h in range(heads):
            at = slice(h * rows, (h + 1) * rows)
            gat[:, at] = ga[at].T

    def score(d, r):
        u = 2 * d + r
        arrived(d, r, 0)

        def body(blk):
            t = dot_nt(ka[u][...], qa[blk]) * (SCALE * LOG2E)
            ts[u][:, blk] = t
            m_s[:, blk] = jnp.maximum(m_s[:, blk], jnp.max(t, axis=0, keepdims=True))

        by_rows(TRF, body)

    def mix(d, r):
        u = 2 * d + r
        arrived(d, r, 1)
        vt[...] = va[u][...].T

        def body(blk):
            m = m_s[:, blk]
            e = jnp.exp2(ts[u][:, blk] - m)
            alpha = jnp.exp2(mo_s[:, blk] - m)
            mo_s[:, blk] = m
            l_s[:, blk] = l_s[:, blk] * alpha + jnp.sum(e, axis=0, keepdims=True)
            ot[:, blk] = ot[:, blk] * alpha + dot_nn(vt[...], e.astype(BF16))

        by_rows(TRF, body)

    def z_in(items):
        wait_recv(z_copy(*item) for item in items)

    wait_recv(t_copy(i, 0) for i in range(1, RANKS))
    start(z_copy(d, r, 0) for r in (0, 1) for d in (1, 3))
    select(0, 0, 0)
    select(0, 1, 0)
    wait_recv(t_copy(i, 1) for i in range(1, RANKS))
    select(0, 0, 1)
    select(0, 1, 1)
    own_fwd()
    score(0, 0)
    z_in([(1, 0, 0), (3, 0, 0)])
    start([z_copy(1, 0, 1), z_copy(3, 0, 1)])
    select(1, 0, 0)
    select(3, 0, 0)
    score(0, 1)
    mix(0, 0)
    z_in([(1, 1, 0), (3, 1, 0)])
    start([z_copy(1, 1, 1), z_copy(3, 1, 1)])
    select(1, 1, 0)
    select(3, 1, 0)
    mix(0, 1)
    turn_grads()
    score(1, 0)
    z_in([(1, 0, 1), (3, 0, 1)])
    start([z_copy(2, 0, 0), z_copy(2, 1, 0)])
    select(1, 0, 1)
    select(3, 0, 1)
    score(3, 0)
    score(1, 1)
    z_in([(1, 1, 1), (3, 1, 1)])
    start([z_copy(2, 0, 1), z_copy(2, 1, 1)])
    select(1, 1, 1)
    select(3, 1, 1)
    score(3, 1)
    mix(1, 0)
    z_in([(2, 0, 0), (2, 1, 0)])
    select(2, 0, 0)
    select(2, 1, 0)
    mix(3, 0)
    mix(1, 1)
    z_in([(2, 0, 1), (2, 1, 1)])
    select(2, 0, 1)
    select(2, 1, 1)
    mix(3, 1)
    score(2, 0)
    score(2, 1)
    mix(2, 0)
    mix(2, 1)

    def stats(blk):
        l = l_s[:, blk]
        o = ot[:, blk] / l
        ot[:, blk] = o
        d_s[:, blk] = jnp.sum(o * gat[:, blk].astype(F32), axis=0, keepdims=True)
        m_s[:, blk] = m_s[:, blk] + jnp.log2(l)
        dqt[:, blk] = jnp.zeros((D, TRF), F32)

    by_rows(TRF, stats)

    def write_out():
        for h in range(heads):
            o = ot[:, h * rows:(h + 1) * rows].T
            o_out[:, h * D:(h + 1) * D] = jnp.where(live, o, 0.0).astype(BF16)
        stores[0].start()

    def bwd_block(t, vs, kts, blk):
        qb, gb = qa[blk], ga[blk]
        p = jnp.exp2(t - m_s[:, blk])
        ds = (p * (dot_nt(vs, gb) - d_s[:, blk])).astype(BF16)
        dv = dot_nn(p.astype(BF16), gb)
        dk = dot_nn(ds, qb)
        dqt[:, blk] += dot_nn(kts, ds)
        return dk, dv

    def bwd(d, r, cuts=1):
        u = 2 * d + r
        kt[...] = ka[u][...].T
        for cut in range(cuts):
            peers = PEERS // cuts
            mine = slice(cut * peers, (cut + 1) * peers)
            keys = slice(cut * peers * BLOCK, (cut + 1) * peers * BLOCK)
            acc_k[keys] = jnp.zeros((peers * BLOCK, D), F32)
            acc_v[keys] = jnp.zeros((peers * BLOCK, D), F32)

            def body(blk):
                dk, dv = bwd_block(ts[u][keys, blk], va[u][keys], kt[:, keys], blk)
                acc_k[keys] += dk
                acc_v[keys] += dv

            by_rows(TRB, body)
            gu[u][mine, 0] = (acc_k[keys] * SCALE).astype(BF16).reshape(peers, BLOCK, D)
            gu[u][mine, 1] = acc_v[keys].astype(BF16).reshape(peers, BLOCK, D)
            start(gx_copy(d, r, j) for j in X_ORDER if j // peers == cut)

    def own_bwd():
        rkt = rk[...].T
        acc_k[:rows] = jnp.zeros((rows, D), F32)
        acc_v[:rows] = jnp.zeros((rows, D), F32)

        def body(blk):
            dk, dv = bwd_block(t_own[:, blk], rv[...], rkt, blk)
            acc_k[:rows] += dk
            acc_v[:rows] += dv

        by_rows(TRB, body)
        drk[...] = (acc_k[:rows] * SCALE).astype(BF16)
        drv[...] = acc_v[:rows].astype(BF16)
        for h in range(heads):
            dq_out[:, h * D:(h + 1) * D] = (dqt[:, h * rows:(h + 1) * rows] * SCALE).T.astype(BF16)
        for copy in stores[1:4]:
            copy.start()

    picks = [[(owners[j] == p).astype(F32) for j in range(PEERS)] for p in range(PROMPTS)]

    def reduce(d, r):
        u = 2 * d + r
        wait_recv(gx_copy(d, r, j) for j in X_ORDER)
        passing = (d, r) in ((1, 0), (3, 1))
        if passing:
            wait_recv([gz_copy(2, r)])

        def body(b, _):
            at = rows_of(b)
            for kv in range(2):
                terms = [gu[u][0, kv, at].astype(F32)] + [rgu[u][j, kv, at].astype(F32) for j in range(1, PEERS)]
                for p in range(PROMPTS):
                    value = terms[0] * picks[p][0]
                    for j in range(1, PEERS):
                        value = value + terms[j] * picks[p][j]
                    if passing:
                        value = value + relay[r][kv, p, at].astype(F32)
                    if d == 0:
                        own_sum[r][kv, p, at] = value
                    else:
                        su[u][kv, p, at] = value.astype(BF16)
            return 0

        lax.fori_loop(0, BLOCK // 16, body, 0)
        if d:
            start([gz_copy(d, r)])

    def finish(r):
        wait_recv(gz_copy(d, r) for d in (1, 3))

        def body(b, _):
            at = rows_of(b)
            for kv in range(2):
                for p in range(PROMPTS):
                    value = own_sum[r][kv, p, at]
                    for d in (1, 3):
                        value = value + rsu[2 * d + r][kv, p, at].astype(F32)
                    bo[r, kv, p, at] = value.astype(BF16)
            return 0

        lax.fori_loop(0, BLOCK // 16, body, 0)
        if comm:
            for k in range(1, 4):
                gt_copy(r, k).start()
            pl.when(zl_at != r)(gt_copy(r, 0).start)

    bwd(2, 0, 2)
    bwd(2, 1)
    bwd(1, 1)
    reduce(2, 0)
    bwd(3, 0)
    reduce(2, 1)
    bwd(1, 0)
    write_out()
    reduce(1, 1)
    bwd(3, 1)
    reduce(3, 0)
    bwd(0, 0)
    reduce(1, 0)
    bwd(0, 1)
    reduce(3, 1)
    own_bwd()
    reduce(0, 0)
    finish(0)
    reduce(0, 1)
    finish(1)
    back[tensor] = bo[tensor // 4, :, :, rows_of(tensor % 4)]

    wait_send(t_copy(i, kv) for i, kv in t_all)
    wait_send(z_copy(d, r, kv) for d in range(1, Z) for r in range(2) for kv in range(2))
    wait_send(x_copy(d, r, kv, j) for d in range(Z) for r in range(2) for kv in range(2) for j in X_ORDER)
    wait_send(gx_copy(d, r, j) for d in range(Z) for r in range(2) for j in X_ORDER)
    wait_send(gz_copy(d, r) for d in range(1, Z) for r in range(2))

    gt_all = [remote(bo.at[0, :, :, rows_of(0)], back.at[0], gt_send.at[i], gt_recv.at[i], (dp, t_peer(i)))
              for i in range(1, RANKS)]
    wait_recv(gt_all)
    for kv in range(2):
        for t in range(RANKS):
            (pk, pv)[kv][:, :, t * D:(t + 1) * D] = jnp.swapaxes(back[t, kv], 0, 1)
        stores[4 + kv].start()
    wait_send(gt_all)
    for copy in stores:
        copy.wait()


def attention(owner, lengths, pk, pv, q, g, rk, rv, comm=True):
    rows, width = q.shape
    total = rows * width // D
    hbm = pl.BlockSpec(memory_space=pl.ANY)
    sm = pl.BlockSpec(memory_space=pltpu.SMEM)
    vmem = pltpu.VMEM
    dma = pltpu.SemaphoreType.DMA
    units = Z * PARTS

    def some(count, shape, dtype=BF16):
        return [vmem(shape, dtype) for _ in range(count)]

    block = (PROMPTS, BLOCK, D)
    scratch = [
        vmem(pk.shape, BF16), vmem(pv.shape, BF16), vmem(q.shape, BF16), vmem(q.shape, BF16),
        vmem(rk.shape, BF16), vmem(rk.shape, BF16), vmem(q.shape, BF16), vmem(q.shape, BF16),
        vmem(rk.shape, BF16), vmem(rk.shape, BF16),
        vmem((RANKS, 2, PROMPTS, 16, D), BF16), vmem((RANKS, 2, PROMPTS, 16, D), BF16),
        vmem((PARTS, *block), BF16), vmem((PARTS, *block), BF16), some(units, block), some(units, block),
        some(units, (PEERS, BLOCK, D)), some(units, (PEERS, BLOCK, D)),
        some(units, (UNIT, D)), some(units, (UNIT, D)),
        some(units, (UNIT, total), F32), vmem((rows, total), F32),
        vmem((total, D), BF16), vmem((total, D), BF16), vmem((D, total), BF16),
        vmem((1, total), F32), vmem((1, total), F32), vmem((1, total), F32), vmem((1, total), F32),
        vmem((D, total), F32), vmem((D, total), F32), vmem((D, UNIT), BF16), vmem((D, UNIT), BF16),
        vmem((UNIT, D), F32), vmem((UNIT, D), F32),
        some(units, (PEERS, 2, BLOCK, D)), some(units, (PEERS, 2, BLOCK, D)),
        some(units, (2, *block)), some(units, (2, *block)), some(PARTS, (2, *block)),
        some(PARTS, (2, *block), F32), vmem((PARTS, 2, *block), BF16),
        dma((12,)), dma((2 * RANKS,)), dma((2 * RANKS,)), dma((2 * units,)), dma((2 * units,)),
        dma((2 * units * PEERS,)), dma((2 * units * PEERS,)), dma((units * PEERS,)), dma((units * PEERS,)),
        dma((units,)), dma((units,)), dma((RANKS,)), dma((RANKS,)),
    ]
    extra = dict(collective_id=0, has_side_effects=True) if comm else {}
    return pl.pallas_call(
        functools.partial(kernel, comm),
        out_shape=(
            jax.ShapeDtypeStruct(q.shape, BF16),
            jax.ShapeDtypeStruct(q.shape, BF16),
            jax.ShapeDtypeStruct(rk.shape, BF16),
            jax.ShapeDtypeStruct(rk.shape, BF16),
            jax.ShapeDtypeStruct(pk.shape, BF16),
            jax.ShapeDtypeStruct(pv.shape, BF16),
        ),
        in_specs=[sm, sm] + [hbm] * 6,
        out_specs=(hbm,) * 6,
        scratch_shapes=scratch,
        compiler_params=pltpu.CompilerParams(vmem_limit_bytes=62 * 2 ** 20, **extra),
    )(owner, lengths, pk, pv, q, g, rk, rv)


def settle_kernel(*refs):
    count = len(refs) // 3
    given, wanted, held = refs[:count], refs[count:2 * count], refs[2 * count:3 * count]
    sems = refs[-1]
    pieces = [(n, slice(at, at + held[n].shape[0] // 2))
              for n in range(count) for at in (0, held[n].shape[0] // 2)]
    loads = [pltpu.make_async_copy(given[n].at[at], held[n].at[at], sems.at[0, i])
             for i, (n, at) in enumerate(pieces)]
    stores = [pltpu.make_async_copy(held[n].at[at], wanted[n].at[at], sems.at[1, i])
              for i, (n, at) in enumerate(pieces)]
    for load in loads:
        load.start()
    for load, store in zip(loads, stores):
        load.wait()
        store.start()
    for store in stores:
        store.wait()


def settle(*arrays):
    hbm = pl.BlockSpec(memory_space=pl.ANY)
    return pl.pallas_call(
        settle_kernel,
        out_shape=tuple(jax.ShapeDtypeStruct(a.shape, a.dtype) for a in arrays),
        in_specs=[hbm] * len(arrays),
        out_specs=(hbm,) * len(arrays),
        scratch_shapes=[pltpu.VMEM(a.shape, a.dtype) for a in arrays]
        + [pltpu.SemaphoreType.DMA((2, 2 * len(arrays)))],
        compiler_params=pltpu.CompilerParams(vmem_limit_bytes=60 * 2 ** 20),
    )(*arrays)


def local(q, rk, rv, prompt_keys, prompt_values, g, lengths, prompt_of):
    return settle(*attention(prompt_of, lengths, prompt_keys, prompt_values, q, g, rk, rv))


def solution(mesh):
    heads = P("dp", "tensor")
    prompt = P(("dp", "tensor"), None, None)
    return jax.shard_map(
        local,
        mesh=mesh,
        in_specs=(heads, heads, heads, prompt, prompt, heads, P("dp"), P()),
        out_specs=(heads, heads, heads, heads, prompt, prompt),
        check_vma=False,
    )
```
